32 devices in a mesh: space: 16 (over z, x, core), filt: 2 (over y).
Axes of the slice: x: 2, y: 2, z: 4, core: 2. Of those that a mesh axis runs over, the one named last changes fastest.
Arguments:
- volume: bfloat16 [32, 32, 32, 128], P('space', 'filt'), may hold values from -6 to 6
- kernel: bfloat16 [3, 3, 3, 256, 128], P(None, None, None, 'filt'), may hold values from -0.109375 to 0.109375
- out_grad: bfloat16 [16, 16, 16, 256], P('space', None, None, 'filt'), may hold values from -6 to 6
Outputs:
- features: bfloat16 [16, 16, 16, 256], P('space', None, None, 'filt')
- in_grad: bfloat16 [32, 32, 32, 128], P('space', 'filt')
- kernel_grad: float32 [3, 3, 3, 256, 128], P(None, None, None, 'filt')
The draws below stay inside these ranges and needn't reach their ends.
All inputs are finite; a program needn't handle non-finite values.
Results may differ from the reference program's by a relative error of at most 0.001.
Values may be sent and summed in bfloat16 or wider, within the bound.
No kernel may reach another device: no remote copies, remote signals or barrier semaphores. Data moves between devices by JAX's collectives and lax.ppermute only.
A program may use at most 64 MiB of HBM per device.

```python
import jax
import jax.numpy as jnp
from jax import lax

CIN = 128
COUT = 256
NZ = 32
NX = 32
NY = 32


def steps_of(own_key, extent, shards, smallest, largest):
    level, own = 1.0, jax.random.fold_in(own_key, 6)
    for position, blocks in shards:
        steps = jnp.exp(jax.random.uniform(jax.random.fold_in(own, position), (blocks,), jnp.float32, smallest / len(shards), largest / len(shards)))
        level = level * jnp.repeat(steps, extent[position] // blocks).reshape([-1 if axis == position else 1 for axis in range(len(extent))])
    return level


def gaussian(own_key, extent, scale, bound, shards=(), held_as=jnp.bfloat16):
    level = steps_of(own_key, extent, shards, -0.22, 0.18) if shards else 1.0
    entries = jax.random.normal(own_key, extent, jnp.float32) * scale * level
    return jnp.minimum(jnp.maximum(entries, -bound), bound).astype(held_as)


def setup_inputs(seed: int = 0) -> dict:
    splits = jax.random.split(jax.random.key(seed), 4)
    volume = gaussian(splits[0], (NX, NY, NZ, CIN), 1.0, 6.0, ((0, 16), (1, 2)))
    kernel = gaussian(splits[1], (3, 3, 3, COUT, CIN), (27 * CIN) ** -0.5, 0.109375, ((3, 2),))
    out_grad = gaussian(splits[2], (NX // 2, NY // 2, NZ // 2, COUT), 1.0, 6.0, ((0, 16), (3, 2)))
    return dict(volume=volume, kernel=kernel, out_grad=out_grad)


def take_patch(padded, a, b, c, dims):
    ox, oy, oz = dims
    chan = padded.shape[3]
    return lax.slice(padded, (a, b, c, 0), (a + 2 * ox - 1, b + 2 * oy - 1, c + 2 * oz - 1, chan), (2, 2, 2, 1))


def reference(volume, kernel, out_grad):
    ox, oy, oz, cout = out_grad.shape
    cin = volume.shape[3]
    dims = (ox, oy, oz)
    padded = jnp.pad(volume, ((1, 1), (1, 1), (1, 1), (0, 0)))
    grad_rows = out_grad.reshape(-1, cout)
    total = jnp.zeros((ox * oy * oz, cout), jnp.float32)
    scatter = jnp.zeros((volume.shape[0] + 2, volume.shape[1] + 2, volume.shape[2] + 2, cin), jnp.float32)
    pieces = []
    for a in range(3):
        for b in range(3):
            for c in range(3):
                patch = take_patch(padded, a, b, c, dims).reshape(-1, cin)
                total = total + lax.dot_general(patch, kernel[a, b, c], (((1,), (1,)), ((), ())), preferred_element_type=jnp.float32)
                pieces.append(lax.dot_general(grad_rows, patch, (((0,), (0,)), ((), ())), preferred_element_type=jnp.float32))
                contrib = jnp.dot(grad_rows, kernel[a, b, c], preferred_element_type=jnp.float32)
                scatter = scatter.at[a:a + 2 * ox - 1:2, b:b + 2 * oy - 1:2, c:c + 2 * oz - 1:2].add(contrib.reshape(ox, oy, oz, cin))
    features = total.reshape(ox, oy, oz, cout).astype(jnp.bfloat16)
    in_grad = scatter[1:-1, 1:-1, 1:-1].astype(jnp.bfloat16)
    factor = float(ox * oy * oz) ** -0.5
    kernel_grad = jnp.stack(pieces).reshape(3, 3, 3, cout, cin) * factor
    return features, in_grad, kernel_grad
```

```python
import functools

import jax
import jax.numpy as jnp
from jax import lax
from jax.experimental import pallas as pl
from jax.experimental.pallas import tpu as pltpu
from jax.sharding import PartitionSpec as P

F32, BF16, F16 = jnp.float32, jnp.bfloat16, jnp.float16
TOP = 15.0
TAPS = 27


def tap(a, b, c):
    return (a * 3 + b) * 3 + c


def uses(parity):
    return ((1, 0),) if parity == 0 else ((2, 0), (0, 1))


def shift_index(dx, dy, dz):
    return (dx * 2 + dy) * 2 + dz


def dot(x, y, dims):
    return lax.dot_general(x, y, (dims, ((), ())), preferred_element_type=F32)


def wide_weights(w_ref, a, b):
    return jnp.concatenate([w_ref[tap(a, b, 1)], w_ref[tap(a, b, 2)]], axis=1)


def grad_kernel(blocks, half, place, g_ref, above_ref, w_ref, gt_ref, part_ref, shifted, cells_of):
    rows, oz, cout = g_ref.shape
    last = lax.broadcasted_iota(jnp.int32, (rows, oz, cout), 1) == oz - 1
    for dx, ref in ((0, g_ref), (1, above_ref)):
        grad = ref[...].astype(F32)
        moved = jnp.where(last, 0.0, pltpu.roll(grad, oz - 1, 1))
        for dz, value in ((0, grad), (1, moved)):
            shifted[dx * 2 + dz, :rows] = value
            shifted[dx * 2 + dz, rows:] = jnp.zeros((1, oz, cout), F32)
    cells = half * oz
    for dx in range(2):
        for dy in range(2):
            for dz in range(2):
                for block in range(blocks):
                    first = place[block] * half + dy
                    piece = shifted[dx * 2 + dz, pl.ds(first, half)].reshape(cells, cout)
                    index = shift_index(dx, dy, dz)
                    span = pl.ds(block * cells, cells)
                    cells_of[index, span] = piece.astype(BF16)
                    gt_ref[index, :, span] = piece.T.astype(BF16)
    cin = w_ref.shape[2]
    for p in range(2):
        for r in range(2):
            total, odd = None, None
            for a, dx in uses(p):
                for b, dy in uses(r):
                    both = dot(cells_of[shift_index(dx, dy, 0)], wide_weights(w_ref, a, b), ((1,), (0,)))
                    late = dot(cells_of[shift_index(dx, dy, 1)], w_ref[tap(a, b, 0)], ((1,), (0,)))
                    total = both if total is None else total + both
                    odd = late if odd is None else odd + late
            parts = (total[:, :cin], total[:, cin:] + odd)
            for block in range(blocks):
                for j in range(half):
                    at = (block * half + j) * oz
                    for q in range(2):
                        part_ref[block, p, 2 * j + r, pl.ds(q, oz, stride=2), :] = parts[q][at : at + oz]


def weight_kernel(blocks, *refs):
    volumes = refs[:blocks]
    gt_ref, sum_ref, class_ref, wide = refs[blocks:]
    planes, rows, depth, cin = volumes[0].shape
    half, oz = rows // 2, depth // 2
    for block in range(blocks):
        wide[...] = volumes[block][...].astype(F32)
        for p in range(2):
            for row in range(rows):
                at = (block * half + row // 2) * oz
                for q in range(2):
                    piece = wide[p, row, pl.ds(q, oz, stride=2), :]
                    class_ref[p * 2 + row % 2, at : at + oz, q * cin : (q + 1) * cin] = piece.astype(BF16)
    largest = None
    for p in range(2):
        for r in range(2):
            patch = class_ref[p * 2 + r]
            for a, dx in uses(p):
                for b, dy in uses(r):
                    both = dot(gt_ref[shift_index(dx, dy, 0)], patch, ((1,), (0,)))
                    late = dot(gt_ref[shift_index(dx, dy, 1)], patch[:, cin:], ((1,), (0,)))
                    for c, term in ((0, late), (1, both[:, :cin]), (2, both[:, cin:])):
                        sum_ref[tap(a, b, c)] = term
                        size = jnp.abs(term)
                        largest = size if largest is None else jnp.maximum(largest, size)
    sum_ref[TAPS] = jnp.maximum(jnp.floor(jnp.log2(largest)) + 1.0, -100.0)


def feature_kernel(blocks, half, place, class_ref, w_ref, own_ref, send_ref, total):
    rows, oz, cout = own_ref.shape
    cin = w_ref.shape[2]
    first_cell = lax.broadcasted_iota(jnp.int32, (rows, oz, cout), 1) == 0
    total[...] = jnp.zeros_like(total)
    for dx in range(2):
        for dy in range(2):
            level, late = None, None
            for p in range(2):
                for a, shift_x in uses(p):
                    for r in range(2):
                        for b, shift_y in uses(r):
                            if (shift_x, shift_y) != (dx, dy):
                                continue
                            patch = class_ref[p * 2 + r]
                            both = dot(patch, wide_weights(w_ref, a, b), ((1,), (1,)))
                            odd = dot(patch[:, cin:], w_ref[tap(a, b, 0)], ((1,), (1,)))
                            level = both if level is None else level + both
                            late = odd if late is None else late + odd
            late = late.reshape(rows, oz, cout)
            level = level.reshape(rows, oz, cout) + jnp.where(first_cell, 0.0, pltpu.roll(late, 1, 1))
            for block in range(blocks):
                where = pl.ds(place[block] * half + dy, half)
                total[dx, where] = total[dx, where] + level[block * half : (block + 1) * half]
    own_ref[...] = total[0, :rows]
    send_ref[...] = total[1, :rows]


def call(kernel, out_shape, arguments, scratch=(), placed=False, flops=0):
    vmem = pl.BlockSpec(memory_space=pltpu.VMEM)
    smem = pl.BlockSpec(memory_space=pltpu.SMEM)
    size = sum(x.size * x.dtype.itemsize for x in list(arguments) + list(out_shape))
    return pl.pallas_call(
        kernel,
        out_shape=out_shape,
        in_specs=[smem if placed and i == 0 else vmem for i in range(len(arguments))],
        out_specs=[vmem] * len(out_shape),
        scratch_shapes=list(scratch),
        compiler_params=pltpu.CompilerParams(vmem_limit_bytes=32 * 1024 * 1024),
        cost_estimate=pl.CostEstimate(flops=flops, bytes_accessed=size, transcendentals=0),
    )(*arguments)


def swap(x, axis, bits):
    peers = lax.axis_size(axis)
    return lax.ppermute(x, axis, [(i, i ^ bits) for i in range(peers)])


def move(x, axis, by):
    peers = lax.axis_size(axis)
    return lax.ppermute(x, axis, [(i, i + by) for i in range(peers) if 0 <= i + by < peers])


def is_level(x):
    return lax.broadcasted_iota(jnp.int32, x.shape, 0) == TAPS


def encode(x):
    return jnp.where(is_level(x), x, x * jnp.exp2(TOP - x[TAPS:])).astype(F16)


def decode(x):
    wide = x.astype(F32)
    return jnp.where(is_level(x), wide, wide * jnp.exp2(wide[TAPS:] - TOP))


def add(x, y):
    return jnp.where(is_level(x), jnp.maximum(x, y) + 1.0, x + y)


def pick(x, index):
    return lax.dynamic_index_in_dim(x, index, 1, keepdims=False)


def arrange(pieces, mine):
    shape = pieces[0].shape[:1] + (len(pieces),) + pieces[0].shape[1:]
    source = lax.broadcasted_iota(jnp.int32, shape, 1) ^ mine
    out = jnp.broadcast_to(pieces[-1][:, None], shape)
    for q in range(len(pieces) - 1):
        out = jnp.where(source == q, jnp.broadcast_to(pieces[q][:, None], shape), out)
    return out


def sum_over_space(terms, factor):
    _, cout, cin = terms.shape
    peers = lax.axis_size("space")
    nz = peers // 4
    index = lax.axis_index("space")
    core, x, z = index & 1, (index >> 1) & 1, index >> 2
    part = terms.reshape(TAPS + 1, 2, 2, nz, cout // peers, cin)
    part = add(pick(part, core), decode(swap(encode(pick(part, 1 - core)), "space", 1)))
    part = add(pick(part, x), decode(swap(encode(pick(part, 1 - x)), "space", 2)))
    got = [swap(encode(pick(part, z ^ q)), "space", 4 * q) for q in range(1, nz)]
    total = pick(part, z)
    for piece in got:
        total = add(total, decode(piece))
    total = encode(jnp.where(is_level(total), total, total * factor))
    total = arrange([total] + [swap(total, "space", 4 * q) for q in range(1, nz)], z)
    total = arrange([total, swap(total, "space", 2)], x)
    total = arrange([total, swap(total, "space", 1)], core)
    return decode(total)[:TAPS].reshape(3, 3, 3, cout, cin)


def on_device(volume, kernel, out_grad):
    planes, rows, depth, cin = volume.shape
    cout = kernel.shape[3]
    filt = lax.axis_size("filt")
    half, oz = rows // 2, depth // 2
    oy = half * filt
    cells = oy * oz
    mine = lax.axis_index("filt")
    if filt == 2:
        volumes = [volume, swap(volume, "filt", 1)]
        place = jnp.stack([mine, 1 - mine]).astype(jnp.int32)
    else:
        gathered = lax.all_gather(volume, "filt", axis=0, tiled=False)
        volumes = [gathered[i] for i in range(filt)]
        place = jnp.arange(filt, dtype=jnp.int32)
    above = move(out_grad, "space", -1)
    weights = kernel.reshape(TAPS, cout, cin)
    flops = 2 * TAPS * cells * cin * cout
    grads, part = call(
        functools.partial(grad_kernel, filt, half),
        [
            jax.ShapeDtypeStruct((8, cout, cells), BF16),
            jax.ShapeDtypeStruct((filt, planes, rows, depth, cin), F32),
        ],
        (place, out_grad[0], above[0], weights),
        [pltpu.VMEM((4, oy + 1, oz, cout), F32), pltpu.VMEM((8, cells, cout), BF16)],
        placed=True,
        flops=flops,
    )
    terms, classes = call(
        functools.partial(weight_kernel, filt),
        [
            jax.ShapeDtypeStruct((TAPS + 1, cout, cin), F32),
            jax.ShapeDtypeStruct((4, cells, 2 * cin), BF16),
        ],
        (*volumes, grads),
        [pltpu.VMEM(volume.shape, F32)],
        flops=flops,
    )
    own, send = call(
        functools.partial(feature_kernel, filt, half),
        [jax.ShapeDtypeStruct((oy, oz, cout), F32)] * 2,
        (place, classes, weights),
        [pltpu.VMEM((2, oy + 1, oz, cout), F32)],
        placed=True,
        flops=flops,
    )
    features = (own + move(send, "space", 1)).astype(BF16)[None]
    if filt == 2:
        gradient = (part[0] + swap(part[1], "filt", 1)).astype(BF16)
    else:
        gradient = lax.psum_scatter(part, "filt", scatter_dimension=0).astype(BF16)
    factor = float(lax.axis_size("space") * cells) ** (-0.5)
    return features, gradient, sum_over_space(terms, factor)


def solution(mesh):
    return jax.shard_map(
        on_device,
        mesh=mesh,
        in_specs=(
            P("space", "filt", None, None),
            P(None, None, None, "filt", None),
            P("space", None, None, "filt"),
        ),
        out_specs=(
            P("space", None, None, "filt"),
            P("space", "filt", None, None),
            P(None, None, None, "filt", None),
        ),
        check_vma=False,
    )
```

```python
import functools

import jax
import jax.numpy as jnp
from jax import lax
from jax.experimental import pallas as pl
from jax.experimental.pallas import tpu as pltpu
from jax.sharding import PartitionSpec as P

F32, BF16, F16 = jnp.float32, jnp.bfloat16, jnp.float16
TOP = 15.0
TAPS = 27


def tap(a, b, c):
    return (a * 3 + b) * 3 + c


def uses(parity):
    return ((1, 0),) if parity == 0 else ((2, 0), (0, 1))


def shift_index(dx, dy, dz):
    return (dx * 2 + dy) * 2 + dz


def dot(x, y, dims):
    return lax.dot_general(x, y, (dims, ((), ())), preferred_element_type=F32)


def wide_weights(w_ref, a, b):
    return jnp.concatenate([w_ref[tap(a, b, 1)], w_ref[tap(a, b, 2)]], axis=1)


def shift_grads(place, half, blocks, levels, shifted, store):
    for level, (dx, ref) in enumerate(levels):
        rows, oz, cout = ref.shape
        last = lax.broadcasted_iota(jnp.int32, (rows, oz, cout), 1) == oz - 1
        grad = ref[...].astype(F32)
        moved = jnp.where(last, 0.0, pltpu.roll(grad, oz - 1, 1))
        for dz, value in ((0, grad), (1, moved)):
            shifted[level * 2 + dz, :rows] = value
            shifted[level * 2 + dz, rows:] = jnp.zeros((1, oz, cout), F32)
    cells = half * oz
    for level, (dx, ref) in enumerate(levels):
        for dy in range(2):
            for dz in range(2):
                for block in range(blocks):
                    first = place[block] * half + dy
                    piece = shifted[level * 2 + dz, pl.ds(first, half)].reshape(cells, cout)
                    store(shift_index(dx, dy, dz), pl.ds(block * cells, cells), piece)


def turn(place, half, blocks, size, g_ref, gt_ref, shifted, turned):
    cout = g_ref.shape[2]
    own = place[blocks]

    def store(index, span, piece):
        turned[...] = piece.T
        order = [turned[pl.ds((own ^ i) * size, size)] for i in range(cout // size)]
        gt_ref[index, :, span] = jnp.concatenate(order, axis=0).astype(BF16)

    shift_grads(place, half, blocks, ((0, g_ref),), shifted, store)


def split_classes(volume_ref, class_ref, wide):
    _, rows, depth, cin = volume_ref.shape
    oz = depth // 2
    wide[...] = volume_ref[...].astype(F32)
    for p in range(2):
        for row in range(rows):
            at = (row // 2) * oz
            for q in range(2):
                piece = wide[p, row, pl.ds(q, oz, stride=2), :]
                class_ref[p * 2 + row % 2, at : at + oz, q * cin : (q + 1) * cin] = piece.astype(BF16)


def own_kernel(blocks, half, size, place, g_ref, volume_ref, gt_ref, class_ref, shifted, turned, wide):
    split_classes(volume_ref, class_ref, wide)
    turn(place, half, blocks, size, g_ref, gt_ref, shifted, turned)


def above_kernel(blocks, half, size, place, g_ref, gt_ref, shifted, turned):
    turn(place, half, blocks, size, g_ref, gt_ref, shifted, turned)


def input_kernel(blocks, half, place, g_ref, above_ref, w_ref, *refs):
    part_refs, (shifted, cells_of) = refs[:blocks], refs[blocks:]
    oz = g_ref.shape[1]

    def store(index, span, piece):
        cells_of[index, span] = piece.astype(BF16)

    shift_grads(place, half, blocks, ((0, g_ref), (1, above_ref)), shifted, store)
    cin = w_ref.shape[2]
    for p in range(2):
        for r in range(2):
            total, odd = None, None
            for a, dx in uses(p):
                for b, dy in uses(r):
                    both = dot(cells_of[shift_index(dx, dy, 0)], wide_weights(w_ref, a, b), ((1,), (0,)))
                    late = dot(cells_of[shift_index(dx, dy, 1)], w_ref[tap(a, b, 0)], ((1,), (0,)))
                    total = both if total is None else total + both
                    odd = late if odd is None else odd + late
            parts = (total[:, :cin], total[:, cin:] + odd)
            for block in range(blocks):
                for j in range(half):
                    at = (block * half + j) * oz
                    for q in range(2):
                        part_refs[block][p, 2 * j + r, pl.ds(q, oz, stride=2), :] = parts[q][at : at + oz]


def weight_kernel(blocks, *refs):
    own_ref, others = refs[0], refs[1:blocks]
    gt0_ref, gt1_ref, near_ref, mid_ref, far_ref, class_ref, wide = refs[blocks:]
    quarter, cin = near_ref.shape[1:]
    cells = own_ref.shape[1]

    def store(index, term):
        near_ref[index] = term[:quarter]
        mid_ref[index] = term[quarter : 2 * quarter]
        far_ref[index] = term[2 * quarter :]

    class_ref[:, :cells] = own_ref[...]
    for block, ref in enumerate(others):
        split_classes(ref, class_ref.at[:, pl.ds((block + 1) * cells, cells)], wide)
    largest = None
    for p in range(2):
        for r in range(2):
            patch = class_ref[p * 2 + r]
            for a, dx in uses(p):
                gt_ref = (gt0_ref, gt1_ref)[dx]
                for b, dy in uses(r):
                    both = dot(gt_ref[shift_index(0, dy, 0)], patch, ((1,), (0,)))
                    late = dot(gt_ref[shift_index(0, dy, 1)], patch[:, cin:], ((1,), (0,)))
                    for c, term in ((0, late), (1, both[:, :cin]), (2, both[:, cin:])):
                        store(tap(a, b, c), term)
                        size = jnp.abs(term)
                        largest = size if largest is None else jnp.maximum(largest, size)
    store(TAPS, jnp.maximum(jnp.floor(jnp.log2(largest)) + 1.0, -100.0))


def feature_kernel(blocks, half, place, class_ref, w_ref, own_ref, send_ref, total):
    rows, oz, cout = own_ref.shape
    cin = w_ref.shape[2]
    first_cell = lax.broadcasted_iota(jnp.int32, (rows, oz, cout), 1) == 0
    total[...] = jnp.zeros_like(total)
    for dx in range(2):
        for dy in range(2):
            level, late = None, None
            for p in range(2):
                for a, shift_x in uses(p):
                    for r in range(2):
                        for b, shift_y in uses(r):
                            if (shift_x, shift_y) != (dx, dy):
                                continue
                            patch = class_ref[p * 2 + r]
                            both = dot(patch, wide_weights(w_ref, a, b), ((1,), (1,)))
                            odd = dot(patch[:, cin:], w_ref[tap(a, b, 0)], ((1,), (1,)))
                            level = both if level is None else level + both
                            late = odd if late is None else late + odd
            late = late.reshape(rows, oz, cout)
            level = level.reshape(rows, oz, cout) + jnp.where(first_cell, 0.0, pltpu.roll(late, 1, 1))
            for block in range(blocks):
                where = pl.ds(place[block] * half + dy, half)
                total[dx, where] = total[dx, where] + level[block * half : (block + 1) * half]
    own_ref[...] = total[0, :rows]
    send_ref[...] = total[1, :rows]


def call(kernel, out_shape, arguments, scratch=(), placed=False, flops=0):
    vmem = pl.BlockSpec(memory_space=pltpu.VMEM)
    smem = pl.BlockSpec(memory_space=pltpu.SMEM)
    size = sum(x.size * x.dtype.itemsize for x in list(arguments) + list(out_shape))
    return pl.pallas_call(
        kernel,
        out_shape=out_shape,
        in_specs=[smem if placed and i == 0 else vmem for i in range(len(arguments))],
        out_specs=[vmem] * len(out_shape),
        scratch_shapes=list(scratch),
        compiler_params=pltpu.CompilerParams(vmem_limit_bytes=8 * 1024 * 1024),
        cost_estimate=pl.CostEstimate(flops=flops, bytes_accessed=size, transcendentals=0),
    )(*arguments)


def swap(x, axis, bits):
    peers = lax.axis_size(axis)
    return lax.ppermute(x, axis, [(i, i ^ bits) for i in range(peers)])


def move(x, axis, by):
    peers = lax.axis_size(axis)
    return lax.ppermute(x, axis, [(i, i + by) for i in range(peers) if 0 <= i + by < peers])


def is_level(x):
    return lax.broadcasted_iota(jnp.int32, x.shape, 0) == TAPS


def encode(x):
    return jnp.where(is_level(x), x, x * jnp.exp2(TOP - x[TAPS:])).astype(F16)


def decode(x):
    return jnp.where(is_level(x), x.astype(F32), x.astype(F32) * jnp.exp2(x[TAPS:].astype(F32) - TOP))


def add(x, y):
    return jnp.where(is_level(x), jnp.maximum(x, y) + 1.0, x + y)


def arrange(pieces, mine):
    shape = pieces[0].shape[:1] + (len(pieces),) + pieces[0].shape[1:]
    source = lax.broadcasted_iota(jnp.int32, shape, 1) ^ mine
    out = jnp.broadcast_to(pieces[-1][:, None], shape)
    for q in range(len(pieces) - 1):
        out = jnp.where(source == q, jnp.broadcast_to(pieces[q][:, None], shape), out)
    return out


def sum_over_space(near, mid, far, where, factor, beside):
    core, x, z, nz = where
    quarter = near.shape[1]
    got = beside("core", swap(encode(far), "space", 1))
    sent = encode(add(mid, decode(got[:, quarter:])))
    near = add(near, decode(got[:, :quarter]))
    got = beside("x", swap(sent, "space", 2))
    total = add(near, decode(got)).reshape(TAPS + 1, nz, quarter // nz, near.shape[2])
    got = [swap(encode(total[:, q]), "space", 4 * q) for q in range(1, nz)]
    total = total[:, 0]
    for piece in got:
        total = add(total, decode(piece))
    total = beside("z", encode(jnp.where(is_level(total), total, total * factor)))
    total = arrange([total] + [swap(total, "space", 4 * q) for q in range(1, nz)], z)
    total = beside("back", total)
    across = beside("end", swap(total, "space", 2))
    cin = near.shape[2]
    out = jnp.zeros((TAPS, 2, 2, nz, quarter // nz, cin), F32)
    pieces = ((core, x, total), (core, 1 - x, across))
    pieces += tuple((1 - core, at, swap(piece, "space", 1)) for _, at, piece in pieces)
    for half, at, piece in pieces:
        out = lax.dynamic_update_slice(out, decode(piece)[:TAPS][:, None, None], (0, half, at, 0, 0, 0))
    return out.reshape(3, 3, 3, 4 * quarter, cin)


def on_device(volume, kernel, out_grad):
    planes, rows, depth, cin = volume.shape
    cout = kernel.shape[3]
    filt = lax.axis_size("filt")
    half, oz = rows // 2, depth // 2
    oy = half * filt
    cells = oy * oz
    mine = lax.axis_index("filt")
    if filt == 2:
        volumes = [volume, swap(volume, "filt", 1)]
        place = [mine, 1 - mine]
    else:
        gathered = lax.all_gather(volume, "filt", axis=0, tiled=False)
        volumes = [gathered[i] for i in range(filt)]
        place = list(range(filt))
    peers = lax.axis_size("space")
    index, nz = lax.axis_index("space"), peers // 4
    core, x, z = index & 1, (index >> 1) & 1, index >> 2
    place = jnp.stack([jnp.asarray(i, jnp.int32) for i in place + [(core * 2 + x) * nz + z]])
    above = move(out_grad, "space", -1)
    weights = kernel.reshape(TAPS, cout, cin)
    flops = 2 * TAPS * cells * cin * cout
    turn_scratch = [pltpu.VMEM((2, oy + 1, oz, cout), F32), pltpu.VMEM((cout, half * oz), F32)]
    own_grads, own_classes = call(
        functools.partial(own_kernel, filt, half, cout // peers),
        [
            jax.ShapeDtypeStruct((4, cout, cells), BF16),
            jax.ShapeDtypeStruct((4, half * oz, 2 * cin), BF16),
        ],
        (place, out_grad[0], volumes[0]),
        turn_scratch + [pltpu.VMEM(volume.shape, F32)],
        placed=True,
    )
    (above_grads,) = call(
        functools.partial(above_kernel, filt, half, cout // peers),
        [jax.ShapeDtypeStruct((4, cout, cells), BF16)],
        (place, above[0]),
        turn_scratch,
        placed=True,
    )
    near, mid, far, classes = call(
        functools.partial(weight_kernel, filt),
        [
            jax.ShapeDtypeStruct((TAPS + 1, cout // 4, cin), F32),
            jax.ShapeDtypeStruct((TAPS + 1, cout // 4, cin), F32),
            jax.ShapeDtypeStruct((TAPS + 1, cout // 2, cin), F32),
            jax.ShapeDtypeStruct((4, cells, 2 * cin), BF16),
        ],
        (own_classes, *volumes[1:], own_grads, above_grads),
        [pltpu.VMEM(volume.shape, F32)],
        flops=flops,
    )
    held = {}

    def beside(stage, value):
        if stage == "core":
            value, gradient, upper = lax.optimization_barrier((value, out_grad, above))
            held["part"] = call(
                functools.partial(input_kernel, filt, half),
                [jax.ShapeDtypeStruct(volume.shape, F32)] * filt,
                (place, gradient[0], upper[0], weights),
                [pltpu.VMEM((4, oy + 1, oz, cout), F32), pltpu.VMEM((8, cells, cout), BF16)],
                placed=True,
                flops=flops,
            )
            held["own"], held["send"] = call(
                functools.partial(feature_kernel, filt, half),
                [jax.ShapeDtypeStruct((oy, oz, cout), F32)] * 2,
                (place, classes, weights),
                [pltpu.VMEM((2, oy + 1, oz, cout), F32)],
                placed=True,
                flops=flops,
            )
            if filt == 2:
                held["in"] = swap(held["part"][1], "filt", 1)
            held["below"] = move(held["send"], "space", 1)
        if stage == "x":
            value, *held["part"], held["own"], held["send"] = lax.optimization_barrier(
                (value, *held["part"], held["own"], held["send"])
            )
        if stage == "end":
            value, held["below"] = lax.optimization_barrier((value, held["below"]))
        if stage == "back" and filt == 2:
            value, held["in"] = lax.optimization_barrier((value, held["in"]))
        return value

    factor = float(peers * cells) ** (-0.5)
    kernel_grad = sum_over_space(near, mid, far, (core, x, z, nz), factor, beside)
    features = (held["own"] + held["below"]).astype(BF16)[None]
    if filt == 2:
        gradient = (held["part"][0] + held["in"]).astype(BF16)
    else:
        gradient = lax.psum_scatter(jnp.stack(held["part"]), "filt", scatter_dimension=0).astype(BF16)
    return features, gradient, kernel_grad


def solution(mesh):
    return jax.shard_map(
        on_device,
        mesh=mesh,
        in_specs=(
            P("space", "filt", None, None),
            P(None, None, None, "filt", None),
            P("space", None, None, "filt"),
        ),
        out_specs=(
            P("space", None, None, "filt"),
            P("space", "filt", None, None),
            P(None, None, None, "filt", None),
        ),
        check_vma=False,
    )
```

```python
import functools

import jax
import jax.numpy as jnp
from jax import lax
from jax.experimental import pallas as pl
from jax.experimental.pallas import tpu as pltpu
from jax.sharding import PartitionSpec as P

F32, BF16, F16 = jnp.float32, jnp.bfloat16, jnp.float16
TOP = 15.0
TAPS = 27


def tap(a, b, c):
    return (a * 3 + b) * 3 + c


def uses(parity):
    return ((1, 0),) if parity == 0 else ((2, 0), (0, 1))


def shift_index(dx, dy, dz):
    return (dx * 2 + dy) * 2 + dz


def dot(x, y, dims):
    return lax.dot_general(x, y, (dims, ((), ())), preferred_element_type=F32)


def wide_weights(w_ref, a, b):
    return jnp.concatenate([w_ref[tap(a, b, 1)], w_ref[tap(a, b, 2)]], axis=1)


def shift_grads(place, half, blocks, levels, shifted, store):
    for level, (dx, ref) in enumerate(levels):
        rows, oz, cout = ref.shape
        last = lax.broadcasted_iota(jnp.int32, (rows, oz, cout), 1) == oz - 1
        grad = ref[...].astype(F32)
        moved = jnp.where(last, 0.0, pltpu.roll(grad, oz - 1, 1))
        for dz, value in ((0, grad), (1, moved)):
            shifted[level * 2 + dz, :rows] = value
            shifted[level * 2 + dz, rows:] = jnp.zeros((1, oz, cout), F32)
    cells = half * oz
    for level, (dx, ref) in enumerate(levels):
        for dy in range(2):
            for dz in range(2):
                for block in range(blocks):
                    first = place[block] * half + dy
                    piece = shifted[level * 2 + dz, pl.ds(first, half)].reshape(cells, cout)
                    store(shift_index(dx, dy, dz), pl.ds(block * cells, cells), piece)


def turn(place, half, blocks, size, g_ref, gt_ref, shifted, turned):
    cout = g_ref.shape[2]
    own = place[blocks]

    def store(index, span, piece):
        turned[...] = piece.T
        order = [turned[pl.ds((own ^ i) * size, size)] for i in range(cout // size)]
        gt_ref[index, :, span] = jnp.concatenate(order, axis=0).astype(BF16)

    shift_grads(place, half, blocks, ((0, g_ref),), shifted, store)


def split_classes(volume_ref, class_ref, wide):
    _, rows, depth, cin = volume_ref.shape
    oz = depth // 2
    wide[...] = volume_ref[...].astype(F32)
    for p in range(2):
        for row in range(rows):
            at = (row // 2) * oz
            for q in range(2):
                piece = wide[p, row, pl.ds(q, oz, stride=2), :]
                class_ref[p * 2 + row % 2, at : at + oz, q * cin : (q + 1) * cin] = piece.astype(BF16)


def own_kernel(blocks, half, size, place, g_ref, volume_ref, gt_ref, class_ref, shifted, turned, wide):
    split_classes(volume_ref, class_ref, wide)
    turn(place, half, blocks, size, g_ref, gt_ref, shifted, turned)


def above_kernel(blocks, half, size, place, g_ref, gt_ref, shifted, turned):
    turn(place, half, blocks, size, g_ref, gt_ref, shifted, turned)


def input_kernel(blocks, half, place, g_ref, above_ref, w_ref, *refs):
    part_refs, (shifted, cells_of) = refs[:blocks], refs[blocks:]
    oz = g_ref.shape[1]

    def store(index, span, piece):
        cells_of[index, span] = piece.astype(BF16)

    shift_grads(place, half, blocks, ((0, g_ref), (1, above_ref)), shifted, store)
    cin = w_ref.shape[2]
    for p in range(2):
        for r in range(2):
            total, odd = None, None
            for a, dx in uses(p):
                for b, dy in uses(r):
                    both = dot(cells_of[shift_index(dx, dy, 0)], wide_weights(w_ref, a, b), ((1,), (0,)))
                    late = dot(cells_of[shift_index(dx, dy, 1)], w_ref[tap(a, b, 0)], ((1,), (0,)))
                    total = both if total is None else total + both
                    odd = late if odd is None else odd + late
            parts = (total[:, :cin], total[:, cin:] + odd)
            for block in range(blocks):
                for j in range(half):
                    at = (block * half + j) * oz
                    for q in range(2):
                        part_refs[block][p, 2 * j + r, pl.ds(q, oz, stride=2), :] = parts[q][at : at + oz]


def weight_kernel(blocks, *refs):
    own_ref, others = refs[0], refs[1:blocks]
    gt0_ref, gt1_ref, near_ref, mid_ref, far_ref, class_ref, wide = refs[blocks:]
    quarter, cin = near_ref.shape[1:]
    cells = own_ref.shape[1]

    def store(index, term):
        near_ref[index] = term[:quarter]
        mid_ref[index] = term[quarter : 2 * quarter]
        far_ref[index] = term[2 * quarter :]

    class_ref[:, :cells] = own_ref[...]
    for block, ref in enumerate(others):
        split_classes(ref, class_ref.at[:, pl.ds((block + 1) * cells, cells)], wide)
    largest = None
    for p in range(2):
        for r in range(2):
            patch = class_ref[p * 2 + r]
            for a, dx in uses(p):
                gt_ref = (gt0_ref, gt1_ref)[dx]
                for b, dy in uses(r):
                    both = dot(gt_ref[shift_index(0, dy, 0)], patch, ((1,), (0,)))
                    late = dot(gt_ref[shift_index(0, dy, 1)], patch[:, cin:], ((1,), (0,)))
                    for c, term in ((0, late), (1, both[:, :cin]), (2, both[:, cin:])):
                        store(tap(a, b, c), term)
                        size = jnp.abs(term)
                        largest = size if largest is None else jnp.maximum(largest, size)
    store(TAPS, jnp.maximum(jnp.floor(jnp.log2(largest)) + 1.0, -100.0))


def feature_kernel(blocks, half, place, class_ref, w_ref, own_ref, send_ref, total):
    rows, oz, cout = own_ref.shape
    cin = w_ref.shape[2]
    first_cell = lax.broadcasted_iota(jnp.int32, (rows, oz, cout), 1) == 0
    total[...] = jnp.zeros_like(total)
    for dx in range(2):
        for dy in range(2):
            level, late = None, None
            for p in range(2):
                for a, shift_x in uses(p):
                    for r in range(2):
                        for b, shift_y in uses(r):
                            if (shift_x, shift_y) != (dx, dy):
                                continue
                            patch = class_ref[p * 2 + r]
                            both = dot(patch, wide_weights(w_ref, a, b), ((1,), (1,)))
                            odd = dot(patch[:, cin:], w_ref[tap(a, b, 0)], ((1,), (1,)))
                            level = both if level is None else level + both
                            late = odd if late is None else late + odd
            late = late.reshape(rows, oz, cout)
            level = level.reshape(rows, oz, cout) + jnp.where(first_cell, 0.0, pltpu.roll(late, 1, 1))
            for block in range(blocks):
                where = pl.ds(place[block] * half + dy, half)
                total[dx, where] = total[dx, where] + level[block * half : (block + 1) * half]
    own_ref[...] = total[0, :rows]
    send_ref[...] = total[1, :rows]


def call(kernel, out_shape, arguments, scratch=(), placed=False, flops=0):
    vmem = pl.BlockSpec(memory_space=pltpu.VMEM)
    smem = pl.BlockSpec(memory_space=pltpu.SMEM)
    size = sum(x.size * x.dtype.itemsize for x in list(arguments) + list(out_shape))
    return pl.pallas_call(
        kernel,
        out_shape=out_shape,
        in_specs=[smem if placed and i == 0 else vmem for i in range(len(arguments))],
        out_specs=[vmem] * len(out_shape),
        scratch_shapes=list(scratch),
        compiler_params=pltpu.CompilerParams(vmem_limit_bytes=8 * 1024 * 1024),
        cost_estimate=pl.CostEstimate(flops=flops, bytes_accessed=size, transcendentals=0),
    )(*arguments)


def swap(x, axis, bits):
    peers = lax.axis_size(axis)
    return lax.ppermute(x, axis, [(i, i ^ bits) for i in range(peers)])


def move(x, axis, by):
    peers = lax.axis_size(axis)
    return lax.ppermute(x, axis, [(i, i + by) for i in range(peers) if 0 <= i + by < peers])


def is_level(x):
    return lax.broadcasted_iota(jnp.int32, x.shape, 0) == TAPS


def encode(x):
    return jnp.where(is_level(x), x, x * jnp.exp2(TOP - x[TAPS:])).astype(F16)


def decode(x):
    return jnp.where(is_level(x), x.astype(F32), x.astype(F32) * jnp.exp2(x[TAPS:].astype(F32) - TOP))


def add(x, y):
    return jnp.where(is_level(x), jnp.maximum(x, y) + 1.0, x + y)


def arrange(pieces, mine):
    shape = pieces[0].shape[:1] + (len(pieces),) + pieces[0].shape[1:]
    source = lax.broadcasted_iota(jnp.int32, shape, 1) ^ mine
    out = jnp.broadcast_to(pieces[-1][:, None], shape)
    for q in range(len(pieces) - 1):
        out = jnp.where(source == q, jnp.broadcast_to(pieces[q][:, None], shape), out)
    return out


def sum_over_space(near, mid, far, where, factor, beside):
    core, x, z, nz = where
    quarter = near.shape[1]
    got = beside("core", swap(encode(far), "space", 1))
    sent = encode(add(mid, decode(got[:, quarter:])))
    near = add(near, decode(got[:, :quarter]))
    got = beside("x", swap(sent, "space", 2))
    total = add(near, decode(got)).reshape(TAPS + 1, nz, quarter // nz, near.shape[2])
    got = [beside(f"z{q}", swap(encode(total[:, q]), "space", 4 * q)) for q in range(1, nz)]
    total = total[:, 0]
    for piece in got:
        total = add(total, decode(piece))
    total = beside("z", encode(jnp.where(is_level(total), total, total * factor)))
    total = arrange([total] + [beside(f"a{q}", swap(total, "space", 4 * q)) for q in range(1, nz)], z)
    total = beside("back", total)
    across = swap(total, "space", 2)
    cin = near.shape[2]
    out = jnp.zeros((TAPS, 2, 2, nz, quarter // nz, cin), F32)
    pieces = ((core, x, total), (core, 1 - x, across))
    pieces += tuple((1 - core, at, beside(f"c{i}", swap(piece, "space", 1))) for i, (_, at, piece) in enumerate(pieces))
    for half, at, piece in pieces:
        out = lax.dynamic_update_slice(out, decode(piece)[:TAPS][:, None, None], (0, half, at, 0, 0, 0))
    return out.reshape(3, 3, 3, 4 * quarter, cin)


def on_device(volume, kernel, out_grad):
    planes, rows, depth, cin = volume.shape
    cout = kernel.shape[3]
    filt = lax.axis_size("filt")
    half, oz = rows // 2, depth // 2
    oy = half * filt
    cells = oy * oz
    mine = lax.axis_index("filt")
    if filt == 2:
        volumes = [volume, swap(volume, "filt", 1)]
        place = [mine, 1 - mine]
    else:
        gathered = lax.all_gather(volume, "filt", axis=0, tiled=False)
        volumes = [gathered[i] for i in range(filt)]
        place = list(range(filt))
    peers = lax.axis_size("space")
    index, nz = lax.axis_index("space"), peers // 4
    core, x, z = index & 1, (index >> 1) & 1, index >> 2
    place = jnp.stack([jnp.asarray(i, jnp.int32) for i in place + [(core * 2 + x) * nz + z]])
    above = move(out_grad, "space", -1)
    weights = kernel.reshape(TAPS, cout, cin)
    flops = 2 * TAPS * cells * cin * cout
    turn_scratch = [pltpu.VMEM((2, oy + 1, oz, cout), F32), pltpu.VMEM((cout, half * oz), F32)]
    own_grads, own_classes = call(
        functools.partial(own_kernel, filt, half, cout // peers),
        [
            jax.ShapeDtypeStruct((4, cout, cells), BF16),
            jax.ShapeDtypeStruct((4, half * oz, 2 * cin), BF16),
        ],
        (place, out_grad[0], volumes[0]),
        turn_scratch + [pltpu.VMEM(volume.shape, F32)],
        placed=True,
    )
    (above_grads,) = call(
        functools.partial(above_kernel, filt, half, cout // peers),
        [jax.ShapeDtypeStruct((4, cout, cells), BF16)],
        (place, above[0]),
        turn_scratch,
        placed=True,
    )
    near, mid, far, classes = call(
        functools.partial(weight_kernel, filt),
        [
            jax.ShapeDtypeStruct((TAPS + 1, cout // 4, cin), F32),
            jax.ShapeDtypeStruct((TAPS + 1, cout // 4, cin), F32),
            jax.ShapeDtypeStruct((TAPS + 1, cout // 2, cin), F32),
            jax.ShapeDtypeStruct((4, cells, 2 * cin), BF16),
        ],
        (own_classes, *volumes[1:], own_grads, above_grads),
        [pltpu.VMEM(volume.shape, F32)],
        flops=flops,
    )
    held = {}

    def beside(stage, value):
        if stage == "core":
            value, gradient, upper = lax.optimization_barrier((value, out_grad, above))
            held["part"] = call(
                functools.partial(input_kernel, filt, half),
                [jax.ShapeDtypeStruct(volume.shape, F32)] * filt,
                (place, gradient[0], upper[0], weights),
                [pltpu.VMEM((4, oy + 1, oz, cout), F32), pltpu.VMEM((8, cells, cout), BF16)],
                placed=True,
                flops=flops,
            )
            held["own"], held["send"] = call(
                functools.partial(feature_kernel, filt, half),
                [jax.ShapeDtypeStruct((oy, oz, cout), F32)] * 2,
                (place, classes, weights),
                [pltpu.VMEM((2, oy + 1, oz, cout), F32)],
                placed=True,
                flops=flops,
            )
        if stage == "x":
            value, *held["part"], held["own"], held["send"] = lax.optimization_barrier(
                (value, *held["part"], held["own"], held["send"])
            )
        if stage == "a2":
            value, held["send"] = lax.optimization_barrier((value, held["send"]))
            held["below"] = move(held["send"], "space", 1)
        if stage == "z3" and filt == 2:
            value, held["part"][1] = lax.optimization_barrier((value, held["part"][1]))
            held["in"] = swap(held["part"][1], "filt", 1)
        if stage == "c1":
            features = (held["own"] + held["below"]).astype(BF16)[None]
            if filt == 2:
                gradient = (held["part"][0] + held["in"]).astype(BF16)
            else:
                gradient = lax.psum_scatter(jnp.stack(held["part"]), "filt", scatter_dimension=0).astype(BF16)
            held["features"], held["gradient"] = features, gradient
            value, held["gradient"] = lax.optimization_barrier((value, gradient))
        return value

    factor = float(peers * cells) ** (-0.5)
    kernel_grad = sum_over_space(near, mid, far, (core, x, z, nz), factor, beside)
    return held["features"], held["gradient"], kernel_grad


def solution(mesh):
    return jax.shard_map(
        on_device,
        mesh=mesh,
        in_specs=(
            P("space", "filt", None, None),
            P(None, None, None, "filt", None),
            P("space", None, None, "filt"),
        ),
        out_specs=(
            P("space", None, None, "filt"),
            P("space", "filt", None, None),
            P(None, None, None, "filt", None),
        ),
        check_vma=False,
    )
```

```python
import functools

import jax
import jax.numpy as jnp
from jax import lax
from jax.experimental import pallas as pl
from jax.experimental.pallas import tpu as pltpu
from jax.sharding import PartitionSpec as P

F32, BF16, F16 = jnp.float32, jnp.bfloat16, jnp.float16
TOP = 15.0
TAPS = 27


def tap(a, b, c):
    return (a * 3 + b) * 3 + c


def uses(parity):
    return ((1, 0),) if parity == 0 else ((2, 0), (0, 1))


def shift_index(dx, dy, dz):
    return (dx * 2 + dy) * 2 + dz


def dot(x, y, dims):
    return lax.dot_general(x, y, (dims, ((), ())), preferred_element_type=F32)


def wide_weights(w_ref, a, b):
    return jnp.concatenate([w_ref[tap(a, b, 1)], w_ref[tap(a, b, 2)]], axis=1)


def shift_grads(place, half, blocks, levels, shifted, store):
    for level, (dx, ref) in enumerate(levels):
        rows, oz, cout = ref.shape
        last = lax.broadcasted_iota(jnp.int32, (rows, oz, cout), 1) == oz - 1
        grad = ref[...].astype(F32)
        moved = jnp.where(last, 0.0, pltpu.roll(grad, oz - 1, 1))
        for dz, value in ((0, grad), (1, moved)):
            shifted[level * 2 + dz, :rows] = value
            shifted[level * 2 + dz, rows:] = jnp.zeros((1, oz, cout), F32)
    cells = half * oz
    for level, (dx, ref) in enumerate(levels):
        for dy in range(2):
            for dz in range(2):
                for block in range(blocks):
                    first = place[block] * half + dy
                    piece = shifted[level * 2 + dz, pl.ds(first, half)].reshape(cells, cout)
                    store(shift_index(dx, dy, dz), pl.ds(block * cells, cells), piece)


def turn(place, half, blocks, size, g_ref, gt_ref, shifted, turned):
    cout = g_ref.shape[2]
    own = place[blocks]

    def store(index, span, piece):
        turned[...] = piece.T
        order = [turned[pl.ds((own ^ i) * size, size)] for i in range(cout // size)]
        gt_ref[index, :, span] = jnp.concatenate(order, axis=0).astype(BF16)

    shift_grads(place, half, blocks, ((0, g_ref),), shifted, store)


def split_classes(volume_ref, class_ref, wide):
    _, rows, depth, cin = volume_ref.shape
    oz = depth // 2
    wide[...] = volume_ref[...].astype(F32)
    for p in range(2):
        for row in range(rows):
            at = (row // 2) * oz
            for q in range(2):
                piece = wide[p, row, pl.ds(q, oz, stride=2), :]
                class_ref[p * 2 + row % 2, at : at + oz, q * cin : (q + 1) * cin] = piece.astype(BF16)


def own_kernel(blocks, half, size, place, g_ref, volume_ref, gt_ref, class_ref, shifted, turned, wide):
    split_classes(volume_ref, class_ref, wide)
    turn(place, half, blocks, size, g_ref, gt_ref, shifted, turned)


def above_kernel(blocks, half, size, place, g_ref, gt_ref, shifted, turned):
    turn(place, half, blocks, size, g_ref, gt_ref, shifted, turned)


def input_kernel(blocks, half, place, g_ref, above_ref, w_ref, *refs):
    part_refs, (shifted, cells_of) = refs[:blocks], refs[blocks:]
    oz = g_ref.shape[1]

    def store(index, span, piece):
        cells_of[index, span] = piece.astype(BF16)

    shift_grads(place, half, blocks, ((0, g_ref), (1, above_ref)), shifted, store)
    cin = w_ref.shape[2]
    for p in range(2):
        for r in range(2):
            total, odd = None, None
            for a, dx in uses(p):
                for b, dy in uses(r):
                    both = dot(cells_of[shift_index(dx, dy, 0)], wide_weights(w_ref, a, b), ((1,), (0,)))
                    late = dot(cells_of[shift_index(dx, dy, 1)], w_ref[tap(a, b, 0)], ((1,), (0,)))
                    total = both if total is None else total + both
                    odd = late if odd is None else odd + late
            parts = (total[:, :cin], total[:, cin:] + odd)
            for block in range(blocks):
                for j in range(half):
                    at = (block * half + j) * oz
                    for q in range(2):
                        part_refs[block][p, 2 * j + r, pl.ds(q, oz, stride=2), :] = parts[q][at : at + oz]


def weight_kernel(blocks, *refs):
    own_ref, others = refs[0], refs[1:blocks]
    gt0_ref, gt1_ref, near_ref, mid_ref, far_ref, class_ref, wide = refs[blocks:]
    quarter, cin = near_ref.shape[1:]
    cells = own_ref.shape[1]

    def store(index, term):
        near_ref[index] = term[:quarter]
        mid_ref[index] = term[quarter : 2 * quarter]
        far_ref[index] = term[2 * quarter :]

    class_ref[:, :cells] = own_ref[...]
    for block, ref in enumerate(others):
        split_classes(ref, class_ref.at[:, pl.ds((block + 1) * cells, cells)], wide)
    largest = None
    for p in range(2):
        for r in range(2):
            patch = class_ref[p * 2 + r]
            for a, dx in uses(p):
                gt_ref = (gt0_ref, gt1_ref)[dx]
                for b, dy in uses(r):
                    both = dot(gt_ref[shift_index(0, dy, 0)], patch, ((1,), (0,)))
                    late = dot(gt_ref[shift_index(0, dy, 1)], patch[:, cin:], ((1,), (0,)))
                    for c, term in ((0, late), (1, both[:, :cin]), (2, both[:, cin:])):
                        store(tap(a, b, c), term)
                        size = jnp.abs(term)
                        largest = size if largest is None else jnp.maximum(largest, size)
    store(TAPS, jnp.maximum(jnp.floor(jnp.log2(largest)) + 1.0, -100.0))


def feature_kernel(blocks, half, place, class_ref, w_ref, own_ref, send_ref, total):
    rows, oz, cout = own_ref.shape
    cin = w_ref.shape[2]
    first_cell = lax.broadcasted_iota(jnp.int32, (rows, oz, cout), 1) == 0
    total[...] = jnp.zeros_like(total)
    for dx in range(2):
        for dy in range(2):
            level, late = None, None
            for p in range(2):
                for a, shift_x in uses(p):
                    for r in range(2):
                        for b, shift_y in uses(r):
                            if (shift_x, shift_y) != (dx, dy):
                                continue
                            patch = class_ref[p * 2 + r]
                            both = dot(patch, wide_weights(w_ref, a, b), ((1,), (1,)))
                            odd = dot(patch[:, cin:], w_ref[tap(a, b, 0)], ((1,), (1,)))
                            level = both if level is None else level + both
                            late = odd if late is None else late + odd
            late = late.reshape(rows, oz, cout)
            level = level.reshape(rows, oz, cout) + jnp.where(first_cell, 0.0, pltpu.roll(late, 1, 1))
            for block in range(blocks):
                where = pl.ds(place[block] * half + dy, half)
                total[dx, where] = total[dx, where] + level[block * half : (block + 1) * half]
    own_ref[...] = total[0, :rows]
    send_ref[...] = total[1, :rows]


def round_kernel(own_ref, below_ref, part_ref, other_ref, features_ref, gradient_ref):
    features_ref[...] = (own_ref[...] + below_ref[...]).astype(BF16)
    gradient_ref[...] = (part_ref[...] + other_ref[...]).astype(BF16)


def call(kernel, out_shape, arguments, scratch=(), placed=False, flops=0):
    vmem = pl.BlockSpec(memory_space=pltpu.VMEM)
    smem = pl.BlockSpec(memory_space=pltpu.SMEM)
    size = sum(x.size * x.dtype.itemsize for x in list(arguments) + list(out_shape))
    return pl.pallas_call(
        kernel,
        out_shape=out_shape,
        in_specs=[smem if placed and i == 0 else vmem for i in range(len(arguments))],
        out_specs=[vmem] * len(out_shape),
        scratch_shapes=list(scratch),
        compiler_params=pltpu.CompilerParams(vmem_limit_bytes=8 * 1024 * 1024),
        cost_estimate=pl.CostEstimate(flops=flops, bytes_accessed=size, transcendentals=0),
    )(*arguments)


def swap(x, axis, bits):
    peers = lax.axis_size(axis)
    return lax.ppermute(x, axis, [(i, i ^ bits) for i in range(peers)])


def move(x, axis, by):
    peers = lax.axis_size(axis)
    return lax.ppermute(x, axis, [(i, i + by) for i in range(peers) if 0 <= i + by < peers])


def is_level(x):
    return lax.broadcasted_iota(jnp.int32, x.shape, 0) == TAPS


def encode(x):
    return jnp.where(is_level(x), x, x * jnp.exp2(TOP - x[TAPS:])).astype(F16)


def decode(x):
    return jnp.where(is_level(x), x.astype(F32), x.astype(F32) * jnp.exp2(x[TAPS:].astype(F32) - TOP))


def add(x, y):
    return jnp.where(is_level(x), jnp.maximum(x, y) + 1.0, x + y)


def arrange(pieces, mine):
    shape = pieces[0].shape[:1] + (len(pieces),) + pieces[0].shape[1:]
    source = lax.broadcasted_iota(jnp.int32, shape, 1) ^ mine
    out = jnp.broadcast_to(pieces[-1][:, None], shape)
    for q in range(len(pieces) - 1):
        out = jnp.where(source == q, jnp.broadcast_to(pieces[q][:, None], shape), out)
    return out


def sum_over_space(near, mid, far, where, factor, beside):
    core, x, z, nz = where
    quarter = near.shape[1]
    got = beside("core", swap(encode(far), "space", 1))
    sent = encode(add(mid, decode(got[:, quarter:])))
    near = add(near, decode(got[:, :quarter]))
    got = beside("x", swap(sent, "space", 2))
    total = add(near, decode(got)).reshape(TAPS + 1, nz, quarter // nz, near.shape[2])
    got = [beside(f"z{q}", swap(encode(total[:, q]), "space", 4 * q)) for q in range(1, nz)]
    total = total[:, 0]
    for piece in got:
        total = add(total, decode(piece))
    total = beside("z", encode(jnp.where(is_level(total), total, total * factor)))
    total = arrange([total] + [beside(f"a{q}", swap(total, "space", 4 * q)) for q in range(1, nz)], z)
    total = beside("back", total)
    across = beside("end", swap(total, "space", 2))
    cin = near.shape[2]
    out = jnp.zeros((TAPS, 2, 2, nz, quarter // nz, cin), F32)
    pieces = ((core, x, total), (core, 1 - x, across))
    pieces += tuple((1 - core, at, beside(f"c{i}", swap(piece, "space", 1))) for i, (_, at, piece) in enumerate(pieces))
    for half, at, piece in pieces:
        out = lax.dynamic_update_slice(out, decode(piece)[:TAPS][:, None, None], (0, half, at, 0, 0, 0))
    return out.reshape(3, 3, 3, 4 * quarter, cin)


def on_device(volume, kernel, out_grad):
    planes, rows, depth, cin = volume.shape
    cout = kernel.shape[3]
    filt = lax.axis_size("filt")
    half, oz = rows // 2, depth // 2
    oy = half * filt
    cells = oy * oz
    mine = lax.axis_index("filt")
    if filt == 2:
        volumes = [volume, swap(volume, "filt", 1)]
        place = [mine, 1 - mine]
    else:
        gathered = lax.all_gather(volume, "filt", axis=0, tiled=False)
        volumes = [gathered[i] for i in range(filt)]
        place = list(range(filt))
    peers = lax.axis_size("space")
    index, nz = lax.axis_index("space"), peers // 4
    core, x, z = index & 1, (index >> 1) & 1, index >> 2
    place = jnp.stack([jnp.asarray(i, jnp.int32) for i in place + [(core * 2 + x) * nz + z]])
    above = move(out_grad, "space", -1)
    weights = kernel.reshape(TAPS, cout, cin)
    flops = 2 * TAPS * cells * cin * cout
    turn_scratch = [pltpu.VMEM((2, oy + 1, oz, cout), F32), pltpu.VMEM((cout, half * oz), F32)]
    own_grads, own_classes = call(
        functools.partial(own_kernel, filt, half, cout // peers),
        [
            jax.ShapeDtypeStruct((4, cout, cells), BF16),
            jax.ShapeDtypeStruct((4, half * oz, 2 * cin), BF16),
        ],
        (place, out_grad[0], volumes[0]),
        turn_scratch + [pltpu.VMEM(volume.shape, F32)],
        placed=True,
    )
    (above_grads,) = call(
        functools.partial(above_kernel, filt, half, cout // peers),
        [jax.ShapeDtypeStruct((4, cout, cells), BF16)],
        (place, above[0]),
        turn_scratch,
        placed=True,
    )
    near, mid, far, classes = call(
        functools.partial(weight_kernel, filt),
        [
            jax.ShapeDtypeStruct((TAPS + 1, cout // 4, cin), F32),
            jax.ShapeDtypeStruct((TAPS + 1, cout // 4, cin), F32),
            jax.ShapeDtypeStruct((TAPS + 1, cout // 2, cin), F32),
            jax.ShapeDtypeStruct((4, cells, 2 * cin), BF16),
        ],
        (own_classes, *volumes[1:], own_grads, above_grads),
        [pltpu.VMEM(volume.shape, F32)],
        flops=flops,
    )
    held = {}

    def beside(stage, value):
        if stage == "core":
            value, gradient, upper = lax.optimization_barrier((value, out_grad, above))
            held["part"] = call(
                functools.partial(input_kernel, filt, half),
                [jax.ShapeDtypeStruct(volume.shape, F32)] * filt,
                (place, gradient[0], upper[0], weights),
                [pltpu.VMEM((4, oy + 1, oz, cout), F32), pltpu.VMEM((8, cells, cout), BF16)],
                placed=True,
                flops=flops,
            )
            held["own"], held["send"] = call(
                functools.partial(feature_kernel, filt, half),
                [jax.ShapeDtypeStruct((oy, oz, cout), F32)] * 2,
                (place, classes, weights),
                [pltpu.VMEM((2, oy + 1, oz, cout), F32)],
                placed=True,
                flops=flops,
            )
        if stage == "x":
            value, *held["part"], held["own"], held["send"] = lax.optimization_barrier(
                (value, *held["part"], held["own"], held["send"])
            )
        if stage == "a2":
            value, held["send"] = lax.optimization_barrier((value, held["send"]))
            held["below"] = move(held["send"], "space", 1)
        if stage == "z3" and filt == 2:
            value, held["part"][1] = lax.optimization_barrier((value, held["part"][1]))
            held["in"] = swap(held["part"][1], "filt", 1)
        if stage == "c1":
            if filt == 2:
                _, below, other = lax.optimization_barrier((value, held["below"], held["in"]))
                held["features"], held["gradient"] = call(
                    round_kernel,
                    [jax.ShapeDtypeStruct(held["own"].shape, BF16), jax.ShapeDtypeStruct(volume.shape, BF16)],
                    (held["own"], below, held["part"][0], other),
                )
            else:
                gradient = lax.psum_scatter(jnp.stack(held["part"]), "filt", scatter_dimension=0)
                held["features"], held["gradient"] = (held["own"] + held["below"]).astype(BF16), gradient.astype(BF16)
        return value

    factor = float(peers * cells) ** (-0.5)
    kernel_grad = sum_over_space(near, mid, far, (core, x, z, nz), factor, beside)
    return held["features"][None], held["gradient"], kernel_grad


def solution(mesh):
    return jax.shard_map(
        on_device,
        mesh=mesh,
        in_specs=(
            P("space", "filt", None, None),
            P(None, None, None, "filt", None),
            P("space", None, None, "filt"),
        ),
        out_specs=(
            P("space", None, None, "filt"),
            P("space", "filt", None, None),
            P(None, None, None, "filt", None),
        ),
        check_vma=False,
    )
```

```python
import functools

import jax
import jax.numpy as jnp
from jax import lax
from jax.experimental import pallas as pl
from jax.experimental.pallas import tpu as pltpu
from jax.sharding import PartitionSpec as P

F32, BF16, F16 = jnp.float32, jnp.bfloat16, jnp.float16
TOP = 15.0
TAPS = 27


def tap(a, b, c):
    return (a * 3 + b) * 3 + c


def uses(parity):
    return ((1, 0),) if parity == 0 else ((2, 0), (0, 1))


def shift_index(dx, dy, dz):
    return (dx * 2 + dy) * 2 + dz


def dot(x, y, dims):
    return lax.dot_general(x, y, (dims, ((), ())), preferred_element_type=F32)


def wide_weights(w_ref, a, b):
    return jnp.concatenate([w_ref[tap(a, b, 1)], w_ref[tap(a, b, 2)]], axis=1)


def shift_grads(place, half, blocks, levels, shifted, store):
    for level, (dx, ref) in enumerate(levels):
        rows, oz, cout = ref.shape
        last = lax.broadcasted_iota(jnp.int32, (rows, oz, cout), 1) == oz - 1
        grad = ref[...].astype(F32)
        moved = jnp.where(last, 0.0, pltpu.roll(grad, oz - 1, 1))
        for dz, value in ((0, grad), (1, moved)):
            shifted[level * 2 + dz, :rows] = value
            shifted[level * 2 + dz, rows:] = jnp.zeros((1, oz, cout), F32)
    cells = half * oz
    for level, (dx, ref) in enumerate(levels):
        for dy in range(2):
            for dz in range(2):
                for block in range(blocks):
                    first = place[block] * half + dy
                    piece = shifted[level * 2 + dz, pl.ds(first, half)].reshape(cells, cout)
                    store(shift_index(dx, dy, dz), pl.ds(block * cells, cells), piece)


def turn(place, half, blocks, size, g_ref, gt_ref, shifted, turned):
    cout = g_ref.shape[2]
    own = place[blocks]

    def store(index, span, piece):
        turned[...] = piece.T
        order = [turned[pl.ds((own ^ i) * size, size)] for i in range(cout // size)]
        gt_ref[index, :, span] = jnp.concatenate(order, axis=0).astype(BF16)

    shift_grads(place, half, blocks, ((0, g_ref),), shifted, store)


def split_classes(volume_ref, class_ref, wide):
    _, rows, depth, cin = volume_ref.shape
    oz = depth // 2
    wide[...] = volume_ref[...].astype(F32)
    for p in range(2):
        for row in range(rows):
            at = (row // 2) * oz
            for q in range(2):
                piece = wide[p, row, pl.ds(q, oz, stride=2), :]
                class_ref[p * 2 + row % 2, at : at + oz, q * cin : (q + 1) * cin] = piece.astype(BF16)


def own_kernel(blocks, half, size, place, g_ref, volume_ref, gt_ref, class_ref, shifted, turned, wide):
    split_classes(volume_ref, class_ref, wide)
    turn(place, half, blocks, size, g_ref, gt_ref, shifted, turned)


def above_kernel(blocks, half, size, place, g_ref, gt_ref, shifted, turned):
    turn(place, half, blocks, size, g_ref, gt_ref, shifted, turned)


def input_kernel(blocks, half, place, g_ref, above_ref, w_ref, *refs):
    part_refs, (shifted, cells_of) = refs[:blocks], refs[blocks:]
    oz = g_ref.shape[1]

    def store(index, span, piece):
        cells_of[index, span] = piece.astype(BF16)

    shift_grads(place, half, blocks, ((0, g_ref), (1, above_ref)), shifted, store)
    cin = w_ref.shape[2]
    for p in range(2):
        for r in range(2):
            total, odd = None, None
            for a, dx in uses(p):
                for b, dy in uses(r):
                    both = dot(cells_of[shift_index(dx, dy, 0)], wide_weights(w_ref, a, b), ((1,), (0,)))
                    late = dot(cells_of[shift_index(dx, dy, 1)], w_ref[tap(a, b, 0)], ((1,), (0,)))
                    total = both if total is None else total + both
                    odd = late if odd is None else odd + late
            parts = (total[:, :cin], total[:, cin:] + odd)
            for block in range(blocks):
                for j in range(half):
                    at = (block * half + j) * oz
                    for q in range(2):
                        part_refs[block][p, 2 * j + r, pl.ds(q, oz, stride=2), :] = parts[q][at : at + oz]


def weight_terms(gt_refs, class_ref, rows, store):
    cin = class_ref.shape[2] // 2
    largest = None
    for p in range(2):
        for r in range(2):
            patch = class_ref[p * 2 + r]
            for a, dx in uses(p):
                for b, dy in uses(r):
                    level, late = [gt_refs[dx][shift_index(0, dy, dz), rows] for dz in range(2)]
                    both = dot(level, patch, ((1,), (0,)))
                    late = dot(late, patch[:, cin:], ((1,), (0,)))
                    for c, term in ((0, late), (1, both[:, :cin]), (2, both[:, cin:])):
                        store(tap(a, b, c), term)
                        size = jnp.abs(term)
                        largest = size if largest is None else jnp.maximum(largest, size)
    store(TAPS, jnp.maximum(jnp.floor(jnp.log2(largest)) + 1.0, -100.0))


def far_kernel(blocks, *refs):
    own_ref, others = refs[0], refs[1:blocks]
    gt0_ref, gt1_ref, far_ref, class_ref, wide = refs[blocks:]
    cells, rows = own_ref.shape[1], far_ref.shape[1]

    def store(index, term):
        far_ref[index] = term

    class_ref[:, :cells] = own_ref[...]
    for block, ref in enumerate(others):
        split_classes(ref, class_ref.at[:, pl.ds((block + 1) * cells, cells)], wide)
    weight_terms((gt0_ref, gt1_ref), class_ref, pl.ds(rows, rows), store)


def home_kernel(class_ref, gt0_ref, gt1_ref, near_ref, mid_ref):
    rows = near_ref.shape[1]

    def store(index, term):
        near_ref[index] = term[:rows]
        mid_ref[index] = term[rows:]

    weight_terms((gt0_ref, gt1_ref), class_ref, pl.ds(0, 2 * rows), store)


def feature_kernel(blocks, half, place, class_ref, w_ref, own_ref, send_ref, total):
    rows, oz, cout = own_ref.shape
    cin = w_ref.shape[2]
    first_cell = lax.broadcasted_iota(jnp.int32, (rows, oz, cout), 1) == 0
    total[...] = jnp.zeros_like(total)
    for dx in range(2):
        for dy in range(2):
            level, late = None, None
            for p in range(2):
                for a, shift_x in uses(p):
                    for r in range(2):
                        for b, shift_y in uses(r):
                            if (shift_x, shift_y) != (dx, dy):
                                continue
                            patch = class_ref[p * 2 + r]
                            both = dot(patch, wide_weights(w_ref, a, b), ((1,), (1,)))
                            odd = dot(patch[:, cin:], w_ref[tap(a, b, 0)], ((1,), (1,)))
                            level = both if level is None else level + both
                            late = odd if late is None else late + odd
            late = late.reshape(rows, oz, cout)
            level = level.reshape(rows, oz, cout) + jnp.where(first_cell, 0.0, pltpu.roll(late, 1, 1))
            for block in range(blocks):
                where = pl.ds(place[block] * half + dy, half)
                total[dx, where] = total[dx, where] + level[block * half : (block + 1) * half]
    own_ref[...] = total[0, :rows]
    send_ref[...] = total[1, :rows]


def round_kernel(own_ref, below_ref, part_ref, other_ref, features_ref, gradient_ref):
    features_ref[...] = (own_ref[...] + below_ref[...]).astype(BF16)
    gradient_ref[...] = (part_ref[...] + other_ref[...]).astype(BF16)


def call(kernel, out_shape, arguments, scratch=(), placed=False, flops=0):
    vmem = pl.BlockSpec(memory_space=pltpu.VMEM)
    smem = pl.BlockSpec(memory_space=pltpu.SMEM)
    size = sum(x.size * x.dtype.itemsize for x in list(arguments) + list(out_shape))
    return pl.pallas_call(
        kernel,
        out_shape=out_shape,
        in_specs=[smem if placed and i == 0 else vmem for i in range(len(arguments))],
        out_specs=[vmem] * len(out_shape),
        scratch_shapes=list(scratch),
        compiler_params=pltpu.CompilerParams(vmem_limit_bytes=8 * 1024 * 1024),
        cost_estimate=pl.CostEstimate(flops=flops, bytes_accessed=size, transcendentals=0),
    )(*arguments)


def swap(x, axis, bits):
    peers = lax.axis_size(axis)
    return lax.ppermute(x, axis, [(i, i ^ bits) for i in range(peers)])


def move(x, axis, by):
    peers = lax.axis_size(axis)
    return lax.ppermute(x, axis, [(i, i + by) for i in range(peers) if 0 <= i + by < peers])


def is_level(x):
    return lax.broadcasted_iota(jnp.int32, x.shape, 0) == TAPS


def encode(x):
    return jnp.where(is_level(x), x, x * jnp.exp2(TOP - x[TAPS:])).astype(F16)


def decode(x):
    return jnp.where(is_level(x), x.astype(F32), x.astype(F32) * jnp.exp2(x[TAPS:].astype(F32) - TOP))


def add(x, y):
    return jnp.where(is_level(x), jnp.maximum(x, y) + 1.0, x + y)


def arrange(pieces, mine):
    shape = pieces[0].shape[:1] + (len(pieces),) + pieces[0].shape[1:]
    source = lax.broadcasted_iota(jnp.int32, shape, 1) ^ mine
    out = jnp.broadcast_to(pieces[-1][:, None], shape)
    for q in range(len(pieces) - 1):
        out = jnp.where(source == q, jnp.broadcast_to(pieces[q][:, None], shape), out)
    return out


def sum_over_space(near, mid, far, where, factor, beside):
    core, x, z, nz = where
    quarter, cin = near.shape[1:]
    shape = (TAPS + 1, nz, quarter // nz, cin)
    got = beside("core", swap(encode(far), "space", 1))
    sent = encode(add(mid, decode(got[:, quarter:]))).reshape(shape)
    near = add(near, decode(got[:, :quarter])).reshape(shape)
    own, got = swap(sent[:, 0], "space", 2), beside("x", swap(sent[:, 1:], "space", 2))
    total = add(near[:, 1:], decode(got))
    got = {q: beside(f"z{q}", swap(encode(total[:, q - 1]), "space", 4 * q)) for q in range(1, nz)}
    got[nz - 1], own = lax.optimization_barrier((got[nz - 1], own))
    total = add(near[:, 0], decode(own))
    for q in got:
        total = add(total, decode(got[q]))
    total = beside("z", encode(jnp.where(is_level(total), total, total * factor)))
    total = arrange([total] + [beside(f"a{q}", swap(total, "space", 4 * q)) for q in range(1, nz)], z)
    total = beside("back", total)
    across = swap(total, "space", 2)
    out = jnp.zeros((TAPS, 2, 2) + shape[1:], F32)
    pieces = ((core, x, total), (core, 1 - x, across))
    pieces += tuple((1 - core, at, beside(f"c{i}", swap(piece, "space", 1))) for i, (_, at, piece) in enumerate(pieces))
    for half, at, piece in pieces:
        out = lax.dynamic_update_slice(out, decode(piece)[:TAPS][:, None, None], (0, half, at, 0, 0, 0))
    return out.reshape(3, 3, 3, 4 * quarter, cin)


def on_device(volume, kernel, out_grad):
    planes, rows, depth, cin = volume.shape
    cout = kernel.shape[3]
    filt = lax.axis_size("filt")
    half, oz = rows // 2, depth // 2
    oy = half * filt
    cells = oy * oz
    mine = lax.axis_index("filt")
    if filt == 2:
        volumes = [volume, swap(volume, "filt", 1)]
        place = [mine, 1 - mine]
    else:
        gathered = lax.all_gather(volume, "filt", axis=0, tiled=False)
        volumes = [gathered[i] for i in range(filt)]
        place = list(range(filt))
    peers = lax.axis_size("space")
    index, nz = lax.axis_index("space"), peers // 4
    core, x, z = index & 1, (index >> 1) & 1, index >> 2
    place = jnp.stack([jnp.asarray(i, jnp.int32) for i in place + [(core * 2 + x) * nz + z]])
    above = move(out_grad, "space", -1)
    weights = kernel.reshape(TAPS, cout, cin)
    flops = 2 * TAPS * cells * cin * cout
    turn_scratch = [pltpu.VMEM((2, oy + 1, oz, cout), F32), pltpu.VMEM((cout, half * oz), F32)]
    own_grads, own_classes = call(
        functools.partial(own_kernel, filt, half, cout // peers),
        [
            jax.ShapeDtypeStruct((4, cout, cells), BF16),
            jax.ShapeDtypeStruct((4, half * oz, 2 * cin), BF16),
        ],
        (place, out_grad[0], volumes[0]),
        turn_scratch + [pltpu.VMEM(volume.shape, F32)],
        placed=True,
    )
    (above_grads,) = call(
        functools.partial(above_kernel, filt, half, cout // peers),
        [jax.ShapeDtypeStruct((4, cout, cells), BF16)],
        (place, above[0]),
        turn_scratch,
        placed=True,
    )
    far, classes = call(
        functools.partial(far_kernel, filt),
        [
            jax.ShapeDtypeStruct((TAPS + 1, cout // 2, cin), F32),
            jax.ShapeDtypeStruct((4, cells, 2 * cin), BF16),
        ],
        (own_classes, *volumes[1:], own_grads, above_grads),
        [pltpu.VMEM(volume.shape, F32)],
        flops=flops // 2,
    )
    near, mid = call(
        home_kernel,
        [jax.ShapeDtypeStruct((TAPS + 1, cout // 4, cin), F32)] * 2,
        (classes, own_grads, above_grads),
        flops=flops // 2,
    )
    held = {}

    def beside(stage, value):
        if stage == "core":
            value, gradient, upper = lax.optimization_barrier((value, out_grad, above))
            held["part"] = call(
                functools.partial(input_kernel, filt, half),
                [jax.ShapeDtypeStruct(volume.shape, F32)] * filt,
                (place, gradient[0], upper[0], weights),
                [pltpu.VMEM((4, oy + 1, oz, cout), F32), pltpu.VMEM((8, cells, cout), BF16)],
                placed=True,
                flops=flops,
            )
            held["own"], held["send"] = call(
                functools.partial(feature_kernel, filt, half),
                [jax.ShapeDtypeStruct((oy, oz, cout), F32)] * 2,
                (place, classes, weights),
                [pltpu.VMEM((2, oy + 1, oz, cout), F32)],
                placed=True,
                flops=flops,
            )
        if stage == "x":
            value, *held["part"], held["own"], held["send"] = lax.optimization_barrier(
                (value, *held["part"], held["own"], held["send"])
            )
        if stage == "a1":
            value, held["send"] = lax.optimization_barrier((value, held["send"]))
            held["below"] = move(held["send"], "space", 1)
        if stage == f"z{nz - 1}" and filt == 2:
            value, held["part"][1] = lax.optimization_barrier((value, held["part"][1]))
            held["in"] = swap(held["part"][1], "filt", 1)
        if stage == "c1":
            if filt == 2:
                _, below, other = lax.optimization_barrier((value, held["below"], held["in"]))
                held["features"], held["gradient"] = call(
                    round_kernel,
                    [jax.ShapeDtypeStruct(held["own"].shape, BF16), jax.ShapeDtypeStruct(volume.shape, BF16)],
                    (held["own"], below, held["part"][0], other),
                )
            else:
                gradient = lax.psum_scatter(jnp.stack(held["part"]), "filt", scatter_dimension=0)
                held["features"], held["gradient"] = (held["own"] + held["below"]).astype(BF16), gradient.astype(BF16)
        return value

    factor = float(peers * cells) ** (-0.5)
    kernel_grad = sum_over_space(near, mid, far, (core, x, z, nz), factor, beside)
    return held["features"][None], held["gradient"], kernel_grad


def solution(mesh):
    return jax.shard_map(
        on_device,
        mesh=mesh,
        in_specs=(
            P("space", "filt", None, None),
            P(None, None, None, "filt", None),
            P("space", None, None, "filt"),
        ),
        out_specs=(
            P("space", None, None, "filt"),
            P("space", "filt", None, None),
            P(None, None, None, "filt", None),
        ),
        check_vma=False,
    )
```

```python
import functools

import jax
import jax.numpy as jnp
from jax import lax
from jax.experimental import pallas as pl
from jax.experimental.pallas import tpu as pltpu
from jax.sharding import PartitionSpec as P

F32, BF16, F16 = jnp.float32, jnp.bfloat16, jnp.float16
TOP = 15.0
TAPS = 27


def tap(a, b, c):
    return (a * 3 + b) * 3 + c


def uses(parity):
    return ((1, 0),) if parity == 0 else ((2, 0), (0, 1))


def shift_index(dx, dy, dz):
    return (dx * 2 + dy) * 2 + dz


def dot(x, y, dims):
    return lax.dot_general(x, y, (dims, ((), ())), preferred_element_type=F32)


def wide_weights(w_ref, a, b):
    return jnp.concatenate([w_ref[tap(a, b, 1)], w_ref[tap(a, b, 2)]], axis=1)


def shift_grads(place, half, blocks, levels, shifted, store):
    for level, (dx, ref) in enumerate(levels):
        rows, oz, cout = ref.shape
        last = lax.broadcasted_iota(jnp.int32, (rows, oz, cout), 1) == oz - 1
        grad = ref[...].astype(F32)
        moved = jnp.where(last, 0.0, pltpu.roll(grad, oz - 1, 1))
        for dz, value in ((0, grad), (1, moved)):
            shifted[level * 2 + dz, :rows] = value
            shifted[level * 2 + dz, rows:] = jnp.zeros((1, oz, cout), F32)
    cells = half * oz
    for level, (dx, ref) in enumerate(levels):
        for dy in range(2):
            for dz in range(2):
                for block in range(blocks):
                    first = place[block] * half + dy
                    piece = shifted[level * 2 + dz, pl.ds(first, half)].reshape(cells, cout)
                    store(shift_index(dx, dy, dz), pl.ds(block * cells, cells), piece)


def turn(place, half, blocks, size, g_ref, gt_ref, shifted, turned):
    cout = g_ref.shape[2]
    own = place[blocks]

    def store(index, span, piece):
        turned[...] = piece.T
        order = [turned[pl.ds((own ^ i) * size, size)] for i in range(cout // size)]
        gt_ref[index, :, span] = jnp.concatenate(order, axis=0).astype(BF16)

    shift_grads(place, half, blocks, ((0, g_ref),), shifted, store)


def split_classes(volume_ref, class_ref, wide):
    _, rows, depth, cin = volume_ref.shape
    oz = depth // 2
    wide[...] = volume_ref[...].astype(F32)
    for p in range(2):
        for row in range(rows):
            at = (row // 2) * oz
            for q in range(2):
                piece = wide[p, row, pl.ds(q, oz, stride=2), :]
                class_ref[p * 2 + row % 2, at : at + oz, q * cin : (q + 1) * cin] = piece.astype(BF16)


def own_kernel(blocks, half, size, place, g_ref, volume_ref, gt_ref, class_ref, shifted, turned, wide):
    split_classes(volume_ref, class_ref, wide)
    turn(place, half, blocks, size, g_ref, gt_ref, shifted, turned)


def above_kernel(blocks, half, size, place, g_ref, gt_ref, shifted, turned):
    turn(place, half, blocks, size, g_ref, gt_ref, shifted, turned)


def input_kernel(blocks, half, place, g_ref, above_ref, w_ref, *refs):
    part_refs, (shifted, cells_of) = refs[:blocks], refs[blocks:]
    oz = g_ref.shape[1]

    def store(index, span, piece):
        cells_of[index, span] = piece.astype(BF16)

    shift_grads(place, half, blocks, ((0, g_ref), (1, above_ref)), shifted, store)
    cin = w_ref.shape[2]
    for p in range(2):
        for r in range(2):
            total, odd = None, None
            for a, dx in uses(p):
                for b, dy in uses(r):
                    both = dot(cells_of[shift_index(dx, dy, 0)], wide_weights(w_ref, a, b), ((1,), (0,)))
                    late = dot(cells_of[shift_index(dx, dy, 1)], w_ref[tap(a, b, 0)], ((1,), (0,)))
                    total = both if total is None else total + both
                    odd = late if odd is None else odd + late
            parts = (total[:, :cin], total[:, cin:] + odd)
            for block in range(blocks):
                for j in range(half):
                    at = (block * half + j) * oz
                    for q in range(2):
                        part_refs[block][p, 2 * j + r, pl.ds(q, oz, stride=2), :] = parts[q][at : at + oz]


def weight_terms(gt_refs, class_ref, rows, store):
    cin = class_ref.shape[2] // 2
    largest = None
    for p in range(2):
        for r in range(2):
            patch = class_ref[p * 2 + r]
            for a, dx in uses(p):
                for b, dy in uses(r):
                    level, late = [gt_refs[dx][shift_index(0, dy, dz), rows] for dz in range(2)]
                    both = dot(level, patch, ((1,), (0,)))
                    late = dot(late, patch[:, cin:], ((1,), (0,)))
                    for c, term in ((0, late), (1, both[:, :cin]), (2, both[:, cin:])):
                        store(tap(a, b, c), term)
                        size = jnp.abs(term)
                        largest = size if largest is None else jnp.maximum(largest, size)
    store(TAPS, jnp.maximum(jnp.floor(jnp.log2(largest)) + 1.0, -100.0))


def far_kernel(blocks, *refs):
    own_ref, others = refs[0], refs[1:blocks]
    gt0_ref, gt1_ref, far_ref, class_ref, wide = refs[blocks:]
    cells, rows = own_ref.shape[1], far_ref.shape[1]

    def store(index, term):
        far_ref[index] = term

    class_ref[:, :cells] = own_ref[...]
    for block, ref in enumerate(others):
        split_classes(ref, class_ref.at[:, pl.ds((block + 1) * cells, cells)], wide)
    weight_terms((gt0_ref, gt1_ref), class_ref, pl.ds(rows, rows), store)


def home_kernel(class_ref, gt0_ref, gt1_ref, near_ref, mid_ref):
    rows = near_ref.shape[1]

    def store(index, term):
        near_ref[index] = term[:rows]
        mid_ref[index] = term[rows:]

    weight_terms((gt0_ref, gt1_ref), class_ref, pl.ds(0, 2 * rows), store)


def feature_kernel(blocks, half, place, class_ref, w_ref, own_ref, send_ref, total):
    rows, oz, cout = own_ref.shape
    cin = w_ref.shape[2]
    first_cell = lax.broadcasted_iota(jnp.int32, (rows, oz, cout), 1) == 0
    total[...] = jnp.zeros_like(total)
    for dx in range(2):
        for dy in range(2):
            level, late = None, None
            for p in range(2):
                for a, shift_x in uses(p):
                    for r in range(2):
                        for b, shift_y in uses(r):
                            if (shift_x, shift_y) != (dx, dy):
                                continue
                            patch = class_ref[p * 2 + r]
                            both = dot(patch, wide_weights(w_ref, a, b), ((1,), (1,)))
                            odd = dot(patch[:, cin:], w_ref[tap(a, b, 0)], ((1,), (1,)))
                            level = both if level is None else level + both
                            late = odd if late is None else late + odd
            late = late.reshape(rows, oz, cout)
            level = level.reshape(rows, oz, cout) + jnp.where(first_cell, 0.0, pltpu.roll(late, 1, 1))
            for block in range(blocks):
                where = pl.ds(place[block] * half + dy, half)
                total[dx, where] = total[dx, where] + level[block * half : (block + 1) * half]
    own_ref[...] = total[0, :rows]
    send_ref[...] = total[1, :rows]


def round_kernel(own_ref, below_ref, part_ref, other_ref, features_ref, gradient_ref):
    features_ref[...] = (own_ref[...] + below_ref[...]).astype(BF16)
    gradient_ref[...] = (part_ref[...] + other_ref[...]).astype(BF16)


def call(kernel, out_shape, arguments, scratch=(), placed=False, flops=0):
    vmem = pl.BlockSpec(memory_space=pltpu.VMEM)
    smem = pl.BlockSpec(memory_space=pltpu.SMEM)
    size = sum(x.size * x.dtype.itemsize for x in list(arguments) + list(out_shape))
    return pl.pallas_call(
        kernel,
        out_shape=out_shape,
        in_specs=[smem if placed and i == 0 else vmem for i in range(len(arguments))],
        out_specs=[vmem] * len(out_shape),
        scratch_shapes=list(scratch),
        compiler_params=pltpu.CompilerParams(vmem_limit_bytes=8 * 1024 * 1024),
        cost_estimate=pl.CostEstimate(flops=flops, bytes_accessed=size, transcendentals=0),
    )(*arguments)


def swap(x, axis, bits):
    peers = lax.axis_size(axis)
    return lax.ppermute(x, axis, [(i, i ^ bits) for i in range(peers)])


def move(x, axis, by):
    peers = lax.axis_size(axis)
    return lax.ppermute(x, axis, [(i, i + by) for i in range(peers) if 0 <= i + by < peers])


def is_level(x):
    return lax.broadcasted_iota(jnp.int32, x.shape, 0) == TAPS


def encode(x):
    return jnp.where(is_level(x), x, x * jnp.exp2(TOP - x[TAPS:])).astype(F16)


def decode(x):
    return jnp.where(is_level(x), x.astype(F32), x.astype(F32) * jnp.exp2(x[TAPS:].astype(F32) - TOP))


def merge(x, arrived, factor=1.0):
    level = x[TAPS:]
    for piece in arrived:
        level = jnp.maximum(level, piece[TAPS:].astype(F32))
    level = level + float(len(arrived))
    total = x * (jnp.exp2(TOP - level) * factor)
    for piece in arrived:
        total = total + piece.astype(F32) * (jnp.exp2(piece[TAPS:].astype(F32) - level) * factor)
    return jnp.where(is_level(x), level, total).astype(F16)


def arrange(pieces, mine):
    shape = pieces[0].shape[:1] + (len(pieces),) + pieces[0].shape[1:]
    source = lax.broadcasted_iota(jnp.int32, shape, 1) ^ mine
    out = jnp.broadcast_to(pieces[-1][:, None], shape)
    for q in range(len(pieces) - 1):
        out = jnp.where(source == q, jnp.broadcast_to(pieces[q][:, None], shape), out)
    return out


def sum_over_space(near, mid, far, where, factor, beside):
    core, x, z, nz = where
    quarter, cin = near.shape[1:]
    shape = (TAPS + 1, nz, quarter // nz, cin)
    got = beside("core", swap(encode(far), "space", 1))
    here, there = jnp.split(got.reshape((TAPS + 1, 2) + shape[1:]), 2, axis=1)
    here, there = here[:, 0], there[:, 0]
    near, mid = near.reshape(shape), mid.reshape(shape)
    sent = merge(mid, [there])
    own, got = swap(sent[:, 0], "space", 2), beside("x", swap(sent[:, 1:], "space", 2))
    ready = {q: merge(near[:, q], [here[:, q], got[:, q - 1]]) for q in range(1, nz)}
    got = {q: beside(f"z{q}", swap(ready[q], "space", 4 * q)) for q in range(1, nz)}
    got[nz - 1], own = lax.optimization_barrier((got[nz - 1], own))
    total = beside("z", merge(near[:, 0], [here[:, 0], own] + [got[q] for q in got], factor))
    total = arrange([total] + [beside(f"a{q}", swap(total, "space", 4 * q)) for q in range(1, nz)], z)
    total = beside("back", total)
    across = swap(total, "space", 2)
    out = jnp.zeros((TAPS, 2, 2) + shape[1:], F32)
    pieces = ((core, x, total), (core, 1 - x, across))
    pieces += tuple((1 - core, at, beside(f"c{i}", swap(piece, "space", 1))) for i, (_, at, piece) in enumerate(pieces))
    for half, at, piece in pieces:
        out = lax.dynamic_update_slice(out, decode(piece)[:TAPS][:, None, None], (0, half, at, 0, 0, 0))
    return out.reshape(3, 3, 3, 4 * quarter, cin)


def on_device(volume, kernel, out_grad):
    planes, rows, depth, cin = volume.shape
    cout = kernel.shape[3]
    filt = lax.axis_size("filt")
    half, oz = rows // 2, depth // 2
    oy = half * filt
    cells = oy * oz
    mine = lax.axis_index("filt")
    if filt == 2:
        volumes = [volume, swap(volume, "filt", 1)]
        place = [mine, 1 - mine]
    else:
        gathered = lax.all_gather(volume, "filt", axis=0, tiled=False)
        volumes = [gathered[i] for i in range(filt)]
        place = list(range(filt))
    peers = lax.axis_size("space")
    index, nz = lax.axis_index("space"), peers // 4
    core, x, z = index & 1, (index >> 1) & 1, index >> 2
    place = jnp.stack([jnp.asarray(i, jnp.int32) for i in place + [(core * 2 + x) * nz + z]])
    above = move(out_grad, "space", -1)
    weights = kernel.reshape(TAPS, cout, cin)
    flops = 2 * TAPS * cells * cin * cout
    turn_scratch = [pltpu.VMEM((2, oy + 1, oz, cout), F32), pltpu.VMEM((cout, half * oz), F32)]
    own_grads, own_classes = call(
        functools.partial(own_kernel, filt, half, cout // peers),
        [
            jax.ShapeDtypeStruct((4, cout, cells), BF16),
            jax.ShapeDtypeStruct((4, half * oz, 2 * cin), BF16),
        ],
        (place, out_grad[0], volumes[0]),
        turn_scratch + [pltpu.VMEM(volume.shape, F32)],
        placed=True,
    )
    (above_grads,) = call(
        functools.partial(above_kernel, filt, half, cout // peers),
        [jax.ShapeDtypeStruct((4, cout, cells), BF16)],
        (place, above[0]),
        turn_scratch,
        placed=True,
    )
    far, classes = call(
        functools.partial(far_kernel, filt),
        [
            jax.ShapeDtypeStruct((TAPS + 1, cout // 2, cin), F32),
            jax.ShapeDtypeStruct((4, cells, 2 * cin), BF16),
        ],
        (own_classes, *volumes[1:], own_grads, above_grads),
        [pltpu.VMEM(volume.shape, F32)],
        flops=flops // 2,
    )
    near, mid = call(
        home_kernel,
        [jax.ShapeDtypeStruct((TAPS + 1, cout // 4, cin), F32)] * 2,
        (classes, own_grads, above_grads),
        flops=flops // 2,
    )
    held = {}

    def beside(stage, value):
        if stage == "core":
            value, gradient, upper = lax.optimization_barrier((value, out_grad, above))
            held["part"] = call(
                functools.partial(input_kernel, filt, half),
                [jax.ShapeDtypeStruct(volume.shape, F32)] * filt,
                (place, gradient[0], upper[0], weights),
                [pltpu.VMEM((4, oy + 1, oz, cout), F32), pltpu.VMEM((8, cells, cout), BF16)],
                placed=True,
                flops=flops,
            )
            held["own"], held["send"] = call(
                functools.partial(feature_kernel, filt, half),
                [jax.ShapeDtypeStruct((oy, oz, cout), F32)] * 2,
                (place, classes, weights),
                [pltpu.VMEM((2, oy + 1, oz, cout), F32)],
                placed=True,
                flops=flops,
            )
        if stage == "x":
            value, *held["part"], held["own"], held["send"] = lax.optimization_barrier(
                (value, *held["part"], held["own"], held["send"])
            )
        if stage == "a1":
            value, held["send"] = lax.optimization_barrier((value, held["send"]))
            held["below"] = move(held["send"], "space", 1)
        if stage == f"z{nz - 1}" and filt == 2:
            value, held["part"][1] = lax.optimization_barrier((value, held["part"][1]))
            held["in"] = swap(held["part"][1], "filt", 1)
        if stage == "c1":
            if filt == 2:
                _, below, other = lax.optimization_barrier((value, held["below"], held["in"]))
                held["features"], held["gradient"] = call(
                    round_kernel,
                    [jax.ShapeDtypeStruct(held["own"].shape, BF16), jax.ShapeDtypeStruct(volume.shape, BF16)],
                    (held["own"], below, held["part"][0], other),
                )
            else:
                gradient = lax.psum_scatter(jnp.stack(held["part"]), "filt", scatter_dimension=0)
                held["features"], held["gradient"] = (held["own"] + held["below"]).astype(BF16), gradient.astype(BF16)
        return value

    factor = float(peers * cells) ** (-0.5)
    kernel_grad = sum_over_space(near, mid, far, (core, x, z, nz), factor, beside)
    return held["features"][None], held["gradient"], kernel_grad


def solution(mesh):
    return jax.shard_map(
        on_device,
        mesh=mesh,
        in_specs=(
            P("space", "filt", None, None),
            P(None, None, None, "filt", None),
            P("space", None, None, "filt"),
        ),
        out_specs=(
            P("space", None, None, "filt"),
            P("space", "filt", None, None),
            P(None, None, None, "filt", None),
        ),
        check_vma=False,
    )
```
